32 devices in a mesh: tm: 8 (over y, x, core), feed: 4 (over z).
Axes of the slice: x: 2, y: 2, z: 4, core: 2. Of those that a mesh axis runs over, the one named last changes fastest.
Arguments:
- voltages: bfloat16 [1024, 16384], P('feed', 'tm'), may hold values from -6 to 6
- coefficients: float32 [16, 2048], replicated, may hold values from -1.5 to 1.5
- beam_weights: bfloat16 [1024, 1024, 2, 512], P('tm', 'feed'), may hold values from -0.1875 to 0.1875
Outputs:
- beam_power: float32 [1, 1024, 512], P(None, 'tm', 'feed')
The draws below stay inside these ranges and needn't reach their ends.
All inputs are finite; a program needn't handle non-finite values.
Results may differ from the reference program's by a relative error of at most 0.0025.
Values may be sent and summed in bfloat16 or wider, within the bound.
A program may use at most 128 MiB of HBM per device.

```python
import math
import jax
import jax.numpy as jnp
from jax import lax

FEEDS = 1024
CH = 1024
BEAMS = 512
TAPS = 16
INTEG = 8
FRAME = 2048
FRAMES = 8
N_TM = 8
N_FEED = 4


def with_spikes(drawn, own_key, source, target, blocks, factor):
    def block_of(position):
        return (jnp.arange(drawn.shape[position]) // (drawn.shape[position] // blocks)).reshape((-1,) + (1,) * (drawn.ndim - 1 - position))

    one_side = jax.random.permutation(own_key, blocks)[block_of(target)]
    far = (block_of(target) + blocks // 2) % blocks
    return jnp.where((block_of(source) == one_side) | (block_of(source) == far), factor * drawn, drawn)


def steps_of(own_key, shape, cuts, least, high):
    factor_of = 1.0
    for position, shards_of in cuts:
        draws = jax.random.uniform(jax.random.fold_in(jax.random.fold_in(own_key, 6), position), (shards_of,), jnp.float32, least / len(cuts), high / len(cuts))
        factor_of = factor_of * jnp.repeat(jnp.exp(draws), shape[position] // shards_of).reshape((-1,) + (1,) * (len(shape) - 1 - position))
    return factor_of


def noise(rng, dims, width, limit, pieces=(), kind=jnp.bfloat16):
    loudness = steps_of(rng, dims, pieces, -0.22, 0.18) if pieces else 1.0
    drawn = jax.random.normal(rng, dims, jnp.float32) * width * loudness
    return jnp.minimum(jnp.maximum(drawn, -limit), limit).astype(kind)


def noise_with(rng, shape, width, bound, split, heavy, kind=jnp.bfloat16):
    drawn = width * jax.random.normal(rng, shape, jnp.float32)
    if split:
        drawn = drawn * steps_of(rng, shape, split, -0.22, 0.18)
    return jnp.clip(with_spikes(drawn, jax.random.fold_in(rng, 3), *heavy), -bound, bound).astype(kind)


def setup_inputs(seed: int = 0) -> dict:
    splits = jax.random.split(jax.random.key(seed), 4)
    return {
        "voltages": noise(splits[0], (FEEDS, FRAMES * FRAME), 1.0, 6.0, ((0, 4), (1, 8))),
        "coefficients": noise(splits[1], (TAPS, FRAME), 0.25, 1.5, (), jnp.float32),
        "beam_weights": noise_with(splits[2], (CH, FEEDS, 2, BEAMS), (2 * FEEDS) ** -0.5, 0.1875, ((0, 8), (1, 4)), (1, 3, 4, 2.0)),
    }


def dft_table(frame_len):
    channels = frame_len // 2
    sample = lax.broadcasted_iota(jnp.int32, (frame_len, channels), 0)
    channel = lax.broadcasted_iota(jnp.int32, (frame_len, channels), 1)
    angles = 2.0 * math.pi / frame_len * (sample * channel % frame_len).astype(jnp.float32)
    norming = 1.0 / math.sqrt(frame_len)
    stacked = jnp.stack([jnp.cos(angles) * norming, -jnp.sin(angles) * norming], axis=2)
    return stacked.reshape(frame_len, 2 * channels).astype(jnp.bfloat16)

def polyphase(extended, coefficients, frames):
    tap_count = coefficients.shape[0]
    running = jnp.zeros((extended.shape[0], frames, extended.shape[2]), jnp.float32)
    for tap_index in range(tap_count):
        running = running + coefficients[tap_index][None, None, :] * extended[:, tap_index:tap_index + frames, :].astype(jnp.float32)
    return running.astype(jnp.bfloat16)

def combine_weights(real_w, imag_w):
    first = jnp.stack([real_w, imag_w], axis=2)
    second = jnp.stack([-imag_w, real_w], axis=2)
    return jnp.stack([first, second], axis=2)

def reference(voltages, coefficients, beam_weights):
    tap_count, frame_len = coefficients.shape
    transform = dft_table(frame_len)
    feed_slab = FEEDS // N_FEED
    grouped = voltages.reshape(N_FEED, feed_slab, FRAMES, frame_len)

    def channelize(feed_block):
        padded = jnp.concatenate([feed_block, jnp.zeros((feed_slab, tap_count - 1, frame_len), jnp.bfloat16)], axis=1)
        filtered = polyphase(padded, coefficients, FRAMES)
        flat = filtered.reshape(feed_slab * FRAMES, frame_len)
        result = jnp.dot(flat, transform, preferred_element_type=jnp.float32).astype(jnp.bfloat16)
        return result.reshape(feed_slab, FRAMES, 2 * CH)
    spectra = lax.map(channelize, grouped).reshape(FEEDS, FRAMES, 2 * CH)
    per_group = CH // N_TM
    arranged = jnp.transpose(spectra.reshape(FEEDS, FRAMES, N_TM, per_group, 2), (2, 1, 3, 4, 0))
    weights_grouped = beam_weights.reshape(N_TM, per_group, FEEDS, 2, BEAMS)

    def form(pair):
        spectrum_block, weight_block = pair
        combined = combine_weights(weight_block[:, :, 0], weight_block[:, :, 1])
        beams = jnp.einsum('tcrf,cfrsb->bsct', spectrum_block.astype(jnp.float32), combined.astype(jnp.float32))
        energy = lax.optimization_barrier(jnp.sum(beams * beams, axis=1))
        binned = lax.optimization_barrier(jnp.mean(energy.reshape(BEAMS, per_group, FRAMES // INTEG, INTEG), axis=3))
        return jnp.transpose(binned, (2, 1, 0))
    powers = lax.map(form, (arranged, weights_grouped))
    return jnp.transpose(powers, (1, 0, 2, 3)).reshape(FRAMES // INTEG, CH, BEAMS)
```

```python
import functools
import math

import jax
import jax.numpy as jnp
import ml_dtypes
import numpy as np
from jax import lax
from jax.experimental import pallas as pl
from jax.experimental.pallas import tpu as pltpu
from jax.sharding import PartitionSpec as P

INTEG = 8


def shifted(value, axis, steps):
    count = lax.axis_size(axis)
    initial, last = (max(0, -steps), min(count, count - steps))
    return lax.ppermute(value, axis, [(source, source + steps) for source in range(initial, last)])


def dft_table(frame_len):
    channels = frame_len // 2
    sample = lax.broadcasted_iota(jnp.int32, (frame_len, channels), 0)
    channel = lax.broadcasted_iota(jnp.int32, (frame_len, channels), 1)
    angles = 2.0 * math.pi / frame_len * (sample * channel % frame_len).astype(jnp.float32)
    norming = 1.0 / math.sqrt(frame_len)
    stacked = jnp.stack([jnp.cos(angles) * norming, -jnp.sin(angles) * norming], axis=2)
    return stacked.reshape(frame_len, 2 * channels).astype(jnp.bfloat16)


def polyphase(extended, coefficients, frames):
    tap_count = coefficients.shape[0]
    running = jnp.zeros((extended.shape[0], frames, extended.shape[2]), jnp.float32)
    for tap_index in range(tap_count):
        running = running + coefficients[tap_index][None, None, :] * extended[
            :, tap_index : tap_index + frames, :
        ].astype(jnp.float32)
    return running.astype(jnp.bfloat16)


def sign_pairs(arranged):
    real_part = arranged[:, :, 0]
    imag_part = arranged[:, :, 1]
    for_real = jnp.stack([real_part, -imag_part], axis=2)
    for_imag = jnp.stack([imag_part, real_part], axis=2)
    return (for_real, for_imag)


def form_beams(for_real, for_imag, weight_part):
    beam_re = jnp.einsum(
        "tcrf,cfrb->bct", for_real, weight_part, preferred_element_type=jnp.float32
    )
    beam_im = jnp.einsum(
        "tcrf,cfrb->bct", for_imag, weight_part, preferred_element_type=jnp.float32
    )
    return jnp.stack([beam_re, beam_im], axis=1)


def detect(beams):
    energy = jnp.sum(beams * beams, axis=1)
    beam_count, per_group, total_frames = energy.shape
    binned = jnp.mean(energy.reshape(beam_count, per_group, total_frames // INTEG, INTEG), axis=3)
    return jnp.transpose(binned, (2, 1, 0))


def general(voltages, coefficients, beam_weights):
    feeds_here, samples = voltages.shape
    tap_count, frame_len = coefficients.shape
    look_ahead = tap_count - 1
    transform = dft_table(frame_len)
    frames = samples // frame_len
    blocks = voltages.reshape(feeds_here, frames, frame_len)
    neighbours = min((look_ahead + frames - 1) // frames, lax.axis_size("tm") - 1)
    pieces = [blocks]
    for distance in range(1, neighbours + 1):
        pieces.append(shifted(blocks, "tm", -distance))
    collected = sum((segment.shape[1] for segment in pieces))
    if collected < frames + look_ahead:
        pieces.append(
            jnp.zeros((feeds_here, frames + look_ahead - collected, frame_len), jnp.bfloat16)
        )
    extended = jnp.concatenate(pieces, axis=1)
    filtered = polyphase(extended, coefficients, frames)
    spectra = jnp.einsum(
        "ftk,kc->tcf", filtered, transform, preferred_element_type=jnp.float32
    ).astype(jnp.bfloat16)
    turned = lax.all_to_all(spectra, "tm", split_axis=1, concat_axis=0, tiled=True)
    total_frames, paired, feed_width = turned.shape
    per_group = paired // 2
    arranged = turned.reshape(total_frames, per_group, 2, feed_width)
    for_real, for_imag = sign_pairs(arranged)
    beams = lax.psum_scatter(
        form_beams(for_real, for_imag, beam_weights), "feed", scatter_dimension=0, tiled=True
    )
    return detect(beams)


def grouped_table(frame_len, groups):
    channels = frame_len // 2
    remainder = (np.arange(frame_len)[:, None] * np.arange(channels)[None, :]) % frame_len
    angles = 2.0 * math.pi / frame_len * remainder
    parts = np.stack([np.cos(angles), -np.sin(angles)], axis=1) / math.sqrt(frame_len)
    split = parts.reshape(frame_len, 2, groups, channels // groups)
    arranged = split.transpose(2, 0, 1, 3).reshape(groups, frame_len, 2 * channels // groups)
    return np.ascontiguousarray(arranged).astype(ml_dtypes.bfloat16)


def greet(axis, n):
    me = lax.axis_index(axis)
    barrier = pltpu.get_barrier_semaphore()
    for k in range(1, n):
        pl.semaphore_signal(
            barrier, inc=1, device_id={axis: lax.rem(me + k, n)}, device_id_type=pl.DeviceIdType.MESH
        )
    pl.semaphore_wait(barrier, n - 1)


def channelize_kernel(
    n, volt, coef, table, out, frames, held, filt, staged, landed,
    table_sem, send1, recv1, send2, recv2,
):
    me = lax.axis_index("tm")
    rows = frames.shape[1]
    taps, frame_len = coef.shape
    fetch = pltpu.make_async_copy(table, held, table_sem)
    fetch.start()
    greet("tm", n)

    def first(k, source):
        dest = lax.rem(me + k, n)
        return pltpu.make_async_remote_copy(
            src_ref=volt.at[pl.ds(pl.multiple_of(dest * rows, rows), rows)],
            dst_ref=frames.at[source],
            send_sem=send1.at[k],
            recv_sem=recv1.at[source],
            device_id={"tm": dest},
            device_id_type=pl.DeviceIdType.MESH,
        )

    for k in range(1, n):
        first(k, me).start()
    frames[me] = volt[pl.ds(pl.multiple_of(me * rows, rows), rows), :]
    for k in range(1, n):
        first(k, lax.rem(me + n - k, n)).wait_recv()

    width = 128

    def columns(step, carry):
        cols = pl.ds(pl.multiple_of(step * width, width), width)
        samples = [frames[t, :, cols].astype(jnp.float32) for t in range(n)]
        for t in range(n):
            running = coef[0:1, cols] * samples[t]
            for p in range(1, min(taps, n - t)):
                running = running + coef[p : p + 1, cols] * samples[t + p]
            filt[t * rows : (t + 1) * rows, cols] = running.astype(jnp.bfloat16)
        return carry

    lax.fori_loop(0, frame_len // width, columns, 0)
    fetch.wait()

    def second(k, source):
        return pltpu.make_async_remote_copy(
            src_ref=staged.at[k],
            dst_ref=landed.at[source],
            send_sem=send2.at[k],
            recv_sem=recv2.at[source],
            device_id={"tm": lax.rem(me + k, n)},
            device_id_type=pl.DeviceIdType.MESH,
        )

    def transform(group):
        return jnp.dot(filt[...], held[group], preferred_element_type=jnp.float32).astype(jnp.bfloat16)

    def send(k, carry):
        staged[k] = transform(lax.rem(me + k, n))
        second(k, me).start()
        return carry

    lax.fori_loop(1, n, send, 0)
    landed[me] = transform(me)
    for k in range(1, n):
        second(k, lax.rem(me + n - k, n)).wait_recv()
    for k in range(1, n):
        first(k, me).wait_send()
        second(k, me).wait_send()
    out[...] = landed[...]


def channelize(voltages, coefficients, n):
    feeds_here, frame_len = voltages.shape
    rows = feeds_here // n
    paired = frame_len // n
    vmem = pl.BlockSpec(memory_space=pltpu.VMEM)
    dma = pltpu.SemaphoreType.DMA
    return pl.pallas_call(
        functools.partial(channelize_kernel, n),
        out_shape=jax.ShapeDtypeStruct((n, n * rows, paired), jnp.bfloat16),
        in_specs=[vmem, vmem, pl.BlockSpec(memory_space=pl.ANY)],
        out_specs=vmem,
        scratch_shapes=[
            pltpu.VMEM((n, rows, frame_len), jnp.bfloat16),
            pltpu.VMEM((n, frame_len, paired), jnp.bfloat16),
            pltpu.VMEM((n * rows, frame_len), jnp.bfloat16),
            pltpu.VMEM((n, n * rows, paired), jnp.bfloat16),
            pltpu.VMEM((n, n * rows, paired), jnp.bfloat16),
            dma, dma((n,)), dma((n,)), dma((n,)), dma((n,)),
        ],
        compiler_params=pltpu.CompilerParams(
            collective_id=0, has_side_effects=True, vmem_limit_bytes=40 << 20
        ),
    )(voltages, coefficients, grouped_table(frame_len, n))


def beams_kernel(n, left, weights, out, formed, own, staged, landed, send_sem, recv_sem):
    step = pl.program_id(0)
    steps = pl.num_programs(0)
    me = lax.axis_index("feed")
    group, feeds_here, _, beams = weights.shape
    share = beams // n

    def copy(k, at):
        block = pl.ds(pl.multiple_of(at * group, group), group)
        return pltpu.make_async_remote_copy(
            src_ref=staged.at[k - 1, block],
            dst_ref=landed.at[k - 1, block],
            send_sem=send_sem.at[k - 1, at],
            recv_sem=recv_sem.at[k - 1, at],
            device_id={"feed": lax.rem(me + k, n)},
            device_id_type=pl.DeviceIdType.MESH,
        )

    @pl.when(step == 0)
    def _():
        greet("feed", n)

    def one(c, carry):
        weight = weights.at[c].reshape(2 * feeds_here, beams)[...]
        formed[c] = jnp.dot(left[c], weight, preferred_element_type=jnp.float32)
        return carry

    lax.fori_loop(0, group, one, 0, unroll=4)
    here = pl.ds(pl.multiple_of(step * group, group), group)
    for k in range(n - 1, 0, -1):
        dest = lax.rem(me + k, n)
        staged[k - 1, here] = formed[
            :, :, pl.ds(pl.multiple_of(dest * share, share), share)
        ].astype(jnp.bfloat16)
        copy(k, step).start()
    own[here] = formed[:, :, pl.ds(pl.multiple_of(me * share, share), share)]

    @pl.when(step == steps - 1)
    def _():
        def finish(at, carry):
            block = pl.ds(pl.multiple_of(at * group, group), group)
            total = own[block]
            for k in range(1, n):
                copy(k, at).wait()
                total = total + landed[k - 1, block].astype(jnp.float32)
            out[block] = jnp.sum(total * total, axis=1) * (1.0 / INTEG)
            return carry

        lax.fori_loop(0, steps, finish, 0)


def beams_power(left, weights, n):
    channels, rows, depth = left.shape
    feeds_here, beams = weights.shape[1], weights.shape[3]
    share = beams // n
    group = 8
    steps = channels // group
    dma = pltpu.SemaphoreType.DMA
    return pl.pallas_call(
        functools.partial(beams_kernel, n),
        grid=(steps,),
        out_shape=jax.ShapeDtypeStruct((channels, share), jnp.float32),
        in_specs=[
            pl.BlockSpec((group, rows, depth), lambda i: (i, 0, 0)),
            pl.BlockSpec((group, feeds_here, 2, beams), lambda i: (i, 0, 0, 0)),
        ],
        out_specs=pl.BlockSpec((channels, share), lambda i: (0, 0)),
        scratch_shapes=[
            pltpu.VMEM((group, rows, beams), jnp.float32),
            pltpu.VMEM((channels, rows, share), jnp.float32),
            pltpu.VMEM((n - 1, channels, rows, share), jnp.bfloat16),
            pltpu.VMEM((n - 1, channels, rows, share), jnp.bfloat16),
            dma((n - 1, steps)), dma((n - 1, steps)),
        ],
        compiler_params=pltpu.CompilerParams(
            collective_id=1, has_side_effects=True, vmem_limit_bytes=40 << 20
        ),
    )(left, weights)


def left_operand(turned, total_frames):
    n, _, paired = turned.shape
    split = turned.reshape(n, total_frames, -1, 2, paired // 2)
    real, imag = split[:, :, :, 0], split[:, :, :, 1]
    pairs = jnp.stack([jnp.stack([real, -imag]), jnp.stack([imag, real])])
    arranged = jnp.transpose(pairs, (5, 0, 3, 2, 4, 1))
    return arranged.reshape(paired // 2, 2 * total_frames, -1)


def fast(voltages, coefficients, beam_weights):
    n_tm, n_feed = lax.axis_size("tm"), lax.axis_size("feed")
    turned = channelize(voltages, coefficients, n_tm)
    left = left_operand(turned, n_tm)
    return beams_power(left, beam_weights, n_feed)[None]


def fits(voltages, coefficients, beam_weights):
    n_tm, n_feed = lax.axis_size("tm"), lax.axis_size("feed")
    feeds_here, samples = voltages.shape
    frame_len = coefficients.shape[1]
    return (
        samples == frame_len
        and n_tm == INTEG
        and feeds_here % (16 * n_tm) == 0
        and frame_len % (256 * n_tm) == 0
        and beam_weights.shape[3] % (128 * n_feed) == 0
    )


def local(voltages, coefficients, beam_weights):
    plan = fast if fits(voltages, coefficients, beam_weights) else general
    return plan(voltages, coefficients, beam_weights)


def solution(mesh):
    placed = (P("feed", "tm"), P(), P("tm", "feed", None, None))
    return jax.shard_map(
        local, mesh=mesh, in_specs=placed, out_specs=P(None, "tm", "feed"), check_vma=False
    )
```

```python
import functools
import math

import jax
import jax.numpy as jnp
import ml_dtypes
import numpy as np
from jax import lax
from jax.experimental import pallas as pl
from jax.experimental.pallas import tpu as pltpu
from jax.sharding import PartitionSpec as P

INTEG = 8


def shifted(value, axis, steps):
    count = lax.axis_size(axis)
    initial, last = (max(0, -steps), min(count, count - steps))
    return lax.ppermute(value, axis, [(source, source + steps) for source in range(initial, last)])


def dft_table(frame_len):
    channels = frame_len // 2
    sample = lax.broadcasted_iota(jnp.int32, (frame_len, channels), 0)
    channel = lax.broadcasted_iota(jnp.int32, (frame_len, channels), 1)
    angles = 2.0 * math.pi / frame_len * (sample * channel % frame_len).astype(jnp.float32)
    norming = 1.0 / math.sqrt(frame_len)
    stacked = jnp.stack([jnp.cos(angles) * norming, -jnp.sin(angles) * norming], axis=2)
    return stacked.reshape(frame_len, 2 * channels).astype(jnp.bfloat16)


def polyphase(extended, coefficients, frames):
    tap_count = coefficients.shape[0]
    running = jnp.zeros((extended.shape[0], frames, extended.shape[2]), jnp.float32)
    for tap_index in range(tap_count):
        running = running + coefficients[tap_index][None, None, :] * extended[
            :, tap_index : tap_index + frames, :
        ].astype(jnp.float32)
    return running.astype(jnp.bfloat16)


def sign_pairs(arranged):
    real_part = arranged[:, :, 0]
    imag_part = arranged[:, :, 1]
    for_real = jnp.stack([real_part, -imag_part], axis=2)
    for_imag = jnp.stack([imag_part, real_part], axis=2)
    return (for_real, for_imag)


def form_beams(for_real, for_imag, weight_part):
    beam_re = jnp.einsum(
        "tcrf,cfrb->bct", for_real, weight_part, preferred_element_type=jnp.float32
    )
    beam_im = jnp.einsum(
        "tcrf,cfrb->bct", for_imag, weight_part, preferred_element_type=jnp.float32
    )
    return jnp.stack([beam_re, beam_im], axis=1)


def detect(beams):
    energy = jnp.sum(beams * beams, axis=1)
    beam_count, per_group, total_frames = energy.shape
    binned = jnp.mean(energy.reshape(beam_count, per_group, total_frames // INTEG, INTEG), axis=3)
    return jnp.transpose(binned, (2, 1, 0))


def general(voltages, coefficients, beam_weights):
    feeds_here, samples = voltages.shape
    tap_count, frame_len = coefficients.shape
    look_ahead = tap_count - 1
    transform = dft_table(frame_len)
    frames = samples // frame_len
    blocks = voltages.reshape(feeds_here, frames, frame_len)
    neighbours = min((look_ahead + frames - 1) // frames, lax.axis_size("tm") - 1)
    pieces = [blocks]
    for distance in range(1, neighbours + 1):
        pieces.append(shifted(blocks, "tm", -distance))
    collected = sum((segment.shape[1] for segment in pieces))
    if collected < frames + look_ahead:
        pieces.append(
            jnp.zeros((feeds_here, frames + look_ahead - collected, frame_len), jnp.bfloat16)
        )
    extended = jnp.concatenate(pieces, axis=1)
    filtered = polyphase(extended, coefficients, frames)
    spectra = jnp.einsum(
        "ftk,kc->tcf", filtered, transform, preferred_element_type=jnp.float32
    ).astype(jnp.bfloat16)
    turned = lax.all_to_all(spectra, "tm", split_axis=1, concat_axis=0, tiled=True)
    total_frames, paired, feed_width = turned.shape
    per_group = paired // 2
    arranged = turned.reshape(total_frames, per_group, 2, feed_width)
    for_real, for_imag = sign_pairs(arranged)
    beams = lax.psum_scatter(
        form_beams(for_real, for_imag, beam_weights), "feed", scatter_dimension=0, tiled=True
    )
    return detect(beams)


def grouped_table(frame_len, groups):
    channels = frame_len // 2
    remainder = (np.arange(frame_len)[:, None] * np.arange(channels)[None, :]) % frame_len
    angles = 2.0 * math.pi / frame_len * remainder
    parts = np.stack([np.cos(angles), -np.sin(angles)], axis=1) / math.sqrt(frame_len)
    split = parts.reshape(frame_len, 2, groups, channels // groups)
    arranged = split.transpose(2, 0, 1, 3).reshape(groups, frame_len, 2 * channels // groups)
    return arranged.astype(ml_dtypes.bfloat16).astype(np.float32)


def greet(axis, n):
    me = lax.axis_index(axis)
    barrier = pltpu.get_barrier_semaphore()
    for k in range(1, n):
        pl.semaphore_signal(
            barrier, inc=1, device_id={axis: lax.rem(me + k, n)}, device_id_type=pl.DeviceIdType.MESH
        )
    pl.semaphore_wait(barrier, n - 1)


def channelize_kernel(
    n, volt, taps_in, table, out, frames, wide, held, filt, staged, landed, coef,
    table_sem, coef_sem, own_sem, send1, recv1, send2, recv2,
):
    me = lax.axis_index("tm")
    rows = frames.shape[1]
    taps, frame_len = coef.shape
    fetch = pltpu.make_async_copy(table, wide, table_sem)
    taps_copy = pltpu.make_async_copy(taps_in, coef, coef_sem)
    own_rows = pl.ds(pl.multiple_of(me * rows, rows), rows)
    own_copy = pltpu.make_async_copy(volt.at[own_rows], frames.at[me], own_sem)
    greet("tm", n)

    def first(k, source):
        dest = lax.rem(me + k, n)
        return pltpu.make_async_remote_copy(
            src_ref=volt.at[pl.ds(pl.multiple_of(dest * rows, rows), rows)],
            dst_ref=frames.at[source],
            send_sem=send1.at[k],
            recv_sem=recv1.at[source],
            device_id={"tm": dest},
            device_id_type=pl.DeviceIdType.MESH,
        )

    for k in range(1, n):
        first(k, me).start()
    own_copy.start()
    taps_copy.start()
    fetch.start()
    fetch.wait()
    chunk = 128
    per = frame_len // chunk

    def narrow(step, carry):
        part = pl.ds(pl.multiple_of(lax.rem(step, per) * chunk, chunk), chunk)
        held[step // per, part] = wide[step // per, part].astype(jnp.bfloat16)
        return carry

    lax.fori_loop(0, n * per, narrow, 0)
    for k in range(1, n):
        first(k, lax.rem(me + n - k, n)).wait_recv()

    own_copy.wait()
    taps_copy.wait()
    width = 128

    def columns(step, carry):
        cols = pl.ds(pl.multiple_of(step * width, width), width)
        samples = [frames[t, :, cols].astype(jnp.float32) for t in range(n)]
        for t in range(n):
            running = coef[0:1, cols] * samples[t]
            for p in range(1, min(taps, n - t)):
                running = running + coef[p : p + 1, cols] * samples[t + p]
            filt[t * rows : (t + 1) * rows, cols] = running.astype(jnp.bfloat16)
        return carry

    lax.fori_loop(0, frame_len // width, columns, 0)

    def second(k, source):
        return pltpu.make_async_remote_copy(
            src_ref=staged.at[k],
            dst_ref=landed.at[source],
            send_sem=send2.at[k],
            recv_sem=recv2.at[source],
            device_id={"tm": lax.rem(me + k, n)},
            device_id_type=pl.DeviceIdType.MESH,
        )

    def transform(group):
        return jnp.dot(filt[...], held[group], preferred_element_type=jnp.float32).astype(jnp.bfloat16)

    def send(k, carry):
        staged[k] = transform(lax.rem(me + k, n))
        second(k, me).start()
        return carry

    lax.fori_loop(1, n, send, 0)
    landed[me] = transform(me)
    for k in range(1, n):
        second(k, lax.rem(me + n - k, n)).wait_recv()
    for k in range(1, n):
        first(k, me).wait_send()
        second(k, me).wait_send()
    out[...] = landed[...]


def channelize(voltages, coefficients, n):
    feeds_here, frame_len = voltages.shape
    rows = feeds_here // n
    paired = frame_len // n
    vmem = pl.BlockSpec(memory_space=pltpu.VMEM)
    dma = pltpu.SemaphoreType.DMA
    return pl.pallas_call(
        functools.partial(channelize_kernel, n),
        out_shape=jax.ShapeDtypeStruct((n, n * rows, paired), jnp.bfloat16),
        in_specs=[pl.BlockSpec(memory_space=pl.ANY)] * 3,
        out_specs=vmem,
        scratch_shapes=[
            pltpu.VMEM((n, rows, frame_len), jnp.bfloat16),
            pltpu.VMEM((n, frame_len, paired), jnp.float32),
            pltpu.VMEM((n, frame_len, paired), jnp.bfloat16),
            pltpu.VMEM((n * rows, frame_len), jnp.bfloat16),
            pltpu.VMEM((n, n * rows, paired), jnp.bfloat16),
            pltpu.VMEM((n, n * rows, paired), jnp.bfloat16),
            pltpu.VMEM(coefficients.shape, jnp.float32),
            dma, dma, dma, dma((n,)), dma((n,)), dma((n,)), dma((n,)),
        ],
        compiler_params=pltpu.CompilerParams(
            collective_id=0, has_side_effects=True, vmem_limit_bytes=60 << 20
        ),
    )(voltages, coefficients, grouped_table(frame_len, n))


def beams_kernel(n, left, weights, out, formed, staged, ahead, behind, send_sem, ahead_sem, behind_sem):
    step = pl.program_id(0)
    steps = pl.num_programs(0)
    me = lax.axis_index("feed")
    group, feeds_here, _, beams = weights.shape
    share = beams // n

    def block(at):
        return pl.ds(pl.multiple_of(at * group, group), group)

    def copy(dest, at, up):
        return pltpu.make_async_remote_copy(
            src_ref=staged.at[dest, block(at)],
            dst_ref=(ahead if up else behind).at[dest, block(at)],
            send_sem=send_sem.at[dest, at],
            recv_sem=(ahead_sem if up else behind_sem).at[dest, at],
            device_id={"feed": jnp.minimum(me + 1, n - 1) if up else jnp.maximum(me - 1, 0)},
            device_id_type=pl.DeviceIdType.MESH,
        )

    def mine(dest, at):
        return formed[block(at), :, dest * share : (dest + 1) * share]

    @pl.when(step == 0)
    def _():
        barrier = pltpu.get_barrier_semaphore()
        for k in range(1, n):
            pl.semaphore_signal(
                barrier, inc=1, device_id={"feed": lax.rem(me + k, n)}, device_id_type=pl.DeviceIdType.MESH
            )
        pl.semaphore_wait(barrier, n - 1)

    def one(c, carry):
        weight = weights.at[c].reshape(2 * feeds_here, beams)[...]
        formed[step * group + c] = jnp.dot(left[c], weight, preferred_element_type=jnp.float32)
        return carry

    lax.fori_loop(0, group, one, 0, unroll=4)

    def begin(dest, at, up):
        staged[dest, block(at)] = mine(dest, at).astype(jnp.bfloat16)
        copy(dest, at, up).start()

    def relay(dest, at, up):
        copy(dest, at, up).wait_recv()
        landed = (ahead if up else behind)[dest, block(at)].astype(jnp.float32)
        staged[dest, block(at)] = (mine(dest, at) + landed).astype(jnp.bfloat16)
        copy(dest, at, up).start()

    @pl.when(me == 0)
    def _():
        for dest in range(n - 1, 0, -1):
            begin(dest, step, True)

    @pl.when(me == n - 1)
    def _():
        for dest in range(n - 1):
            begin(dest, step, False)

    def pass_on(at):
        for dest in range(n - 1, 1, -1):
            @pl.when((me > 0) & (dest > me))
            def _():
                relay(dest, at, True)

        for dest in range(n - 2):
            @pl.when((me < n - 1) & (dest < me))
            def _():
                relay(dest, at, False)

    lag = 2

    @pl.when(step >= lag)
    def _():
        pass_on(step - lag)

    @pl.when(step == steps - 1)
    def _():
        for back in range(lag, 0, -1):
            pass_on(steps - back)

        def finish(at, carry):
            for dest in range(n):
                @pl.when(dest < me)
                def _():
                    copy(dest, at, False).wait_send()

                @pl.when(dest > me)
                def _():
                    copy(dest, at, True).wait_send()

                @pl.when(dest == me)
                def _():
                    formed[block(at), :, :share] = mine(dest, at)

            @pl.when(me > 0)
            def _():
                copy(me, at, True).wait_recv()
                formed[block(at), :, :share] = formed[block(at), :, :share] + ahead[me, block(at)].astype(jnp.float32)

            @pl.when(me < n - 1)
            def _():
                copy(me, at, False).wait_recv()
                formed[block(at), :, :share] = formed[block(at), :, :share] + behind[me, block(at)].astype(jnp.float32)

            total = formed[block(at), :, :share]
            out[block(at)] = jnp.sum(total * total, axis=1) * (1.0 / INTEG)
            return carry

        lax.fori_loop(0, steps, finish, 0)


def beams_power(left, weights, n):
    channels, rows, depth = left.shape
    feeds_here, beams = weights.shape[1], weights.shape[3]
    share = beams // n
    group = 8
    steps = channels // group
    dma = pltpu.SemaphoreType.DMA
    slots = pltpu.VMEM((n, channels, rows, share), jnp.bfloat16)
    return pl.pallas_call(
        functools.partial(beams_kernel, n),
        grid=(steps,),
        out_shape=jax.ShapeDtypeStruct((channels, share), jnp.float32),
        in_specs=[
            pl.BlockSpec((group, rows, depth), lambda i: (i, 0, 0)),
            pl.BlockSpec((group, feeds_here, 2, beams), lambda i: (i, 0, 0, 0)),
        ],
        out_specs=pl.BlockSpec((channels, share), lambda i: (0, 0)),
        scratch_shapes=[
            pltpu.VMEM((channels, rows, beams), jnp.float32),
            slots, slots, slots,
            dma((n, steps)), dma((n, steps)), dma((n, steps)),
        ],
        compiler_params=pltpu.CompilerParams(
            collective_id=1, has_side_effects=True, vmem_limit_bytes=40 << 20
        ),
    )(left, weights)


def left_operand(turned, total_frames):
    n, _, paired = turned.shape
    split = turned.reshape(n, total_frames, -1, 2, paired // 2)
    real, imag = split[:, :, :, 0], split[:, :, :, 1]
    pairs = jnp.stack([jnp.stack([real, -imag]), jnp.stack([imag, real])])
    arranged = jnp.transpose(pairs, (5, 0, 3, 2, 4, 1))
    return arranged.reshape(paired // 2, 2 * total_frames, -1)


def fast(voltages, coefficients, beam_weights):
    n_tm, n_feed = lax.axis_size("tm"), lax.axis_size("feed")
    turned = channelize(voltages, coefficients, n_tm)
    left = left_operand(turned, n_tm)
    return beams_power(left, beam_weights, n_feed)[None]


def fits(voltages, coefficients, beam_weights):
    n_tm, n_feed = lax.axis_size("tm"), lax.axis_size("feed")
    feeds_here, samples = voltages.shape
    frame_len = coefficients.shape[1]
    return (
        samples == frame_len
        and n_tm == INTEG
        and feeds_here % (16 * n_tm) == 0
        and frame_len % (256 * n_tm) == 0
        and beam_weights.shape[3] % (128 * n_feed) == 0
    )


def local(voltages, coefficients, beam_weights):
    plan = fast if fits(voltages, coefficients, beam_weights) else general
    return plan(voltages, coefficients, beam_weights)


def solution(mesh):
    placed = (P("feed", "tm"), P(), P("tm", "feed", None, None))
    return jax.shard_map(
        local, mesh=mesh, in_specs=placed, out_specs=P(None, "tm", "feed"), check_vma=False
    )
```

```python
import functools
import math

import jax
import jax.numpy as jnp
import ml_dtypes
import numpy as np
from jax import lax
from jax.experimental import pallas as pl
from jax.experimental.pallas import tpu as pltpu
from jax.sharding import PartitionSpec as P

INTEG = 8


def shifted(value, axis, steps):
    count = lax.axis_size(axis)
    initial, last = (max(0, -steps), min(count, count - steps))
    return lax.ppermute(value, axis, [(source, source + steps) for source in range(initial, last)])


def dft_table(frame_len):
    channels = frame_len // 2
    sample = lax.broadcasted_iota(jnp.int32, (frame_len, channels), 0)
    channel = lax.broadcasted_iota(jnp.int32, (frame_len, channels), 1)
    angles = 2.0 * math.pi / frame_len * (sample * channel % frame_len).astype(jnp.float32)
    norming = 1.0 / math.sqrt(frame_len)
    stacked = jnp.stack([jnp.cos(angles) * norming, -jnp.sin(angles) * norming], axis=2)
    return stacked.reshape(frame_len, 2 * channels).astype(jnp.bfloat16)


def polyphase(extended, coefficients, frames):
    tap_count = coefficients.shape[0]
    running = jnp.zeros((extended.shape[0], frames, extended.shape[2]), jnp.float32)
    for tap_index in range(tap_count):
        running = running + coefficients[tap_index][None, None, :] * extended[
            :, tap_index : tap_index + frames, :
        ].astype(jnp.float32)
    return running.astype(jnp.bfloat16)


def sign_pairs(arranged):
    real_part = arranged[:, :, 0]
    imag_part = arranged[:, :, 1]
    for_real = jnp.stack([real_part, -imag_part], axis=2)
    for_imag = jnp.stack([imag_part, real_part], axis=2)
    return (for_real, for_imag)


def form_beams(for_real, for_imag, weight_part):
    beam_re = jnp.einsum(
        "tcrf,cfrb->bct", for_real, weight_part, preferred_element_type=jnp.float32
    )
    beam_im = jnp.einsum(
        "tcrf,cfrb->bct", for_imag, weight_part, preferred_element_type=jnp.float32
    )
    return jnp.stack([beam_re, beam_im], axis=1)


def detect(beams):
    energy = jnp.sum(beams * beams, axis=1)
    beam_count, per_group, total_frames = energy.shape
    binned = jnp.mean(energy.reshape(beam_count, per_group, total_frames // INTEG, INTEG), axis=3)
    return jnp.transpose(binned, (2, 1, 0))


def general(voltages, coefficients, beam_weights):
    feeds_here, samples = voltages.shape
    tap_count, frame_len = coefficients.shape
    look_ahead = tap_count - 1
    transform = dft_table(frame_len)
    frames = samples // frame_len
    blocks = voltages.reshape(feeds_here, frames, frame_len)
    neighbours = min((look_ahead + frames - 1) // frames, lax.axis_size("tm") - 1)
    pieces = [blocks]
    for distance in range(1, neighbours + 1):
        pieces.append(shifted(blocks, "tm", -distance))
    collected = sum((segment.shape[1] for segment in pieces))
    if collected < frames + look_ahead:
        pieces.append(
            jnp.zeros((feeds_here, frames + look_ahead - collected, frame_len), jnp.bfloat16)
        )
    extended = jnp.concatenate(pieces, axis=1)
    filtered = polyphase(extended, coefficients, frames)
    spectra = jnp.einsum(
        "ftk,kc->tcf", filtered, transform, preferred_element_type=jnp.float32
    ).astype(jnp.bfloat16)
    turned = lax.all_to_all(spectra, "tm", split_axis=1, concat_axis=0, tiled=True)
    total_frames, paired, feed_width = turned.shape
    per_group = paired // 2
    arranged = turned.reshape(total_frames, per_group, 2, feed_width)
    for_real, for_imag = sign_pairs(arranged)
    beams = lax.psum_scatter(
        form_beams(for_real, for_imag, beam_weights), "feed", scatter_dimension=0, tiled=True
    )
    return detect(beams)


def grouped_table(frame_len, groups):
    channels = frame_len // 2
    remainder = (np.arange(frame_len)[:, None] * np.arange(channels)[None, :]) % frame_len
    angles = 2.0 * math.pi / frame_len * remainder
    parts = np.stack([np.cos(angles), -np.sin(angles)], axis=1) / math.sqrt(frame_len)
    split = parts.reshape(frame_len, 2, groups, channels // groups)
    arranged = split.transpose(2, 0, 1, 3).reshape(groups, frame_len, 2 * channels // groups)
    return arranged.astype(ml_dtypes.bfloat16).astype(np.float32)


def greet(axis, n):
    me = lax.axis_index(axis)
    barrier = pltpu.get_barrier_semaphore()
    for k in range(1, n):
        pl.semaphore_signal(
            barrier, inc=1, device_id={axis: lax.rem(me + k, n)}, device_id_type=pl.DeviceIdType.MESH
        )
    pl.semaphore_wait(barrier, n - 1)


def channelize_kernel(
    n, volt, taps_in, table, out, frames, wide, held, filt, staged, landed, coef,
    table_sem, coef_sem, own_sem, send1, recv1, send2, recv2,
):
    me = lax.axis_index("tm")
    rows = frames.shape[1]
    taps, frame_len = coef.shape
    fetch = pltpu.make_async_copy(table, wide, table_sem)
    taps_copy = pltpu.make_async_copy(taps_in, coef, coef_sem)
    own_rows = pl.ds(pl.multiple_of(me * rows, rows), rows)
    own_copy = pltpu.make_async_copy(volt.at[own_rows], frames.at[me], own_sem)
    greet("tm", n)

    def first(k, source):
        dest = lax.rem(me + k, n)
        return pltpu.make_async_remote_copy(
            src_ref=volt.at[pl.ds(pl.multiple_of(dest * rows, rows), rows)],
            dst_ref=frames.at[source],
            send_sem=send1.at[k],
            recv_sem=recv1.at[source],
            device_id={"tm": dest},
            device_id_type=pl.DeviceIdType.MESH,
        )

    for k in range(1, n):
        first(k, me).start()
    own_copy.start()
    taps_copy.start()
    fetch.start()
    fetch.wait()
    chunk = 128
    per = frame_len // chunk

    def narrow(step, carry):
        part = pl.ds(pl.multiple_of(lax.rem(step, per) * chunk, chunk), chunk)
        held[step // per, part] = wide[step // per, part].astype(jnp.bfloat16)
        return carry

    lax.fori_loop(0, n * per, narrow, 0)
    for k in range(1, n):
        first(k, lax.rem(me + n - k, n)).wait_recv()

    own_copy.wait()
    taps_copy.wait()
    width = 128

    def columns(step, carry):
        cols = pl.ds(pl.multiple_of(step * width, width), width)
        samples = [frames[t, :, cols].astype(jnp.float32) for t in range(n)]
        for t in range(n):
            running = coef[0:1, cols] * samples[t]
            for p in range(1, min(taps, n - t)):
                running = running + coef[p : p + 1, cols] * samples[t + p]
            filt[t * rows : (t + 1) * rows, cols] = running.astype(jnp.bfloat16)
        return carry

    lax.fori_loop(0, frame_len // width, columns, 0)

    def second(k, source):
        return pltpu.make_async_remote_copy(
            src_ref=staged.at[k],
            dst_ref=landed.at[source],
            send_sem=send2.at[k],
            recv_sem=recv2.at[source],
            device_id={"tm": lax.rem(me + k, n)},
            device_id_type=pl.DeviceIdType.MESH,
        )

    def transform(group):
        return jnp.dot(filt[...], held[group], preferred_element_type=jnp.float32).astype(jnp.bfloat16)

    def send(k, carry):
        staged[k] = transform(lax.rem(me + k, n))
        second(k, me).start()
        return carry

    lax.fori_loop(1, n, send, 0)
    landed[me] = transform(me)
    for k in range(1, n):
        second(k, lax.rem(me + n - k, n)).wait_recv()
    for k in range(1, n):
        first(k, me).wait_send()
        second(k, me).wait_send()
    out[...] = landed[...]


def channelize(voltages, coefficients, n):
    feeds_here, frame_len = voltages.shape
    rows = feeds_here // n
    paired = frame_len // n
    vmem = pl.BlockSpec(memory_space=pltpu.VMEM)
    dma = pltpu.SemaphoreType.DMA
    return pl.pallas_call(
        functools.partial(channelize_kernel, n),
        out_shape=jax.ShapeDtypeStruct((n, n * rows, paired), jnp.bfloat16),
        in_specs=[pl.BlockSpec(memory_space=pl.ANY)] * 3,
        out_specs=vmem,
        scratch_shapes=[
            pltpu.VMEM((n, rows, frame_len), jnp.bfloat16),
            pltpu.VMEM((n, frame_len, paired), jnp.float32),
            pltpu.VMEM((n, frame_len, paired), jnp.bfloat16),
            pltpu.VMEM((n * rows, frame_len), jnp.bfloat16),
            pltpu.VMEM((n, n * rows, paired), jnp.bfloat16),
            pltpu.VMEM((n, n * rows, paired), jnp.bfloat16),
            pltpu.VMEM(coefficients.shape, jnp.float32),
            dma, dma, dma, dma((n,)), dma((n,)), dma((n,)), dma((n,)),
        ],
        compiler_params=pltpu.CompilerParams(
            collective_id=0, has_side_effects=True, vmem_limit_bytes=60 << 20
        ),
    )(voltages, coefficients, grouped_table(frame_len, n))


def beams_kernel(n, left, weights, out, formed, own, staged, landed, send_sem, recv_sem):
    step = pl.program_id(0)
    steps = pl.num_programs(0)
    me = lax.axis_index("feed")
    group, feeds_here, _, beams = weights.shape
    share = beams // n

    def copy(k, at):
        block = pl.ds(pl.multiple_of(at * group, group), group)
        return pltpu.make_async_remote_copy(
            src_ref=staged.at[k - 1, block],
            dst_ref=landed.at[k - 1, block],
            send_sem=send_sem.at[k - 1, at],
            recv_sem=recv_sem.at[k - 1, at],
            device_id={"feed": lax.rem(me + k, n)},
            device_id_type=pl.DeviceIdType.MESH,
        )

    @pl.when(step == 0)
    def _():
        greet("feed", n)

    def one(c, carry):
        weight = weights.at[c].reshape(2 * feeds_here, beams)[...]
        formed[c] = jnp.dot(left[c], weight, preferred_element_type=jnp.float32)
        return carry

    lax.fori_loop(0, group, one, 0, unroll=4)
    here = pl.ds(pl.multiple_of(step * group, group), group)
    for k in range(n - 1, 0, -1):
        dest = lax.rem(me + k, n)
        staged[k - 1, here] = formed[
            :, :, pl.ds(pl.multiple_of(dest * share, share), share)
        ].astype(jnp.bfloat16)
        copy(k, step).start()
    own[here] = formed[:, :, pl.ds(pl.multiple_of(me * share, share), share)]

    @pl.when(step == steps - 1)
    def _():
        def finish(at, carry):
            block = pl.ds(pl.multiple_of(at * group, group), group)
            total = own[block]
            for k in range(1, n):
                copy(k, at).wait()
                total = total + landed[k - 1, block].astype(jnp.float32)
            out[block] = jnp.sum(total * total, axis=1) * (1.0 / INTEG)
            return carry

        lax.fori_loop(0, steps, finish, 0)


def beams_power(left, weights, n):
    channels, rows, depth = left.shape
    feeds_here, beams = weights.shape[1], weights.shape[3]
    share = beams // n
    group = 8
    steps = channels // group
    dma = pltpu.SemaphoreType.DMA
    return pl.pallas_call(
        functools.partial(beams_kernel, n),
        grid=(steps,),
        out_shape=jax.ShapeDtypeStruct((channels, share), jnp.float32),
        in_specs=[
            pl.BlockSpec((group, rows, depth), lambda i: (i, 0, 0)),
            pl.BlockSpec((group, feeds_here, 2, beams), lambda i: (i, 0, 0, 0)),
        ],
        out_specs=pl.BlockSpec((channels, share), lambda i: (0, 0)),
        scratch_shapes=[
            pltpu.VMEM((group, rows, beams), jnp.float32),
            pltpu.VMEM((channels, rows, share), jnp.float32),
            pltpu.VMEM((n - 1, channels, rows, share), jnp.bfloat16),
            pltpu.VMEM((n - 1, channels, rows, share), jnp.bfloat16),
            dma((n - 1, steps)), dma((n - 1, steps)),
        ],
        compiler_params=pltpu.CompilerParams(
            collective_id=1, has_side_effects=True, vmem_limit_bytes=40 << 20
        ),
    )(left, weights)


def left_operand(turned, total_frames):
    n, _, paired = turned.shape
    split = turned.reshape(n, total_frames, -1, 2, paired // 2)
    real, imag = split[:, :, :, 0], split[:, :, :, 1]
    pairs = jnp.stack([jnp.stack([real, -imag]), jnp.stack([imag, real])])
    arranged = jnp.transpose(pairs, (5, 0, 3, 2, 4, 1))
    return arranged.reshape(paired // 2, 2 * total_frames, -1)


def fast(voltages, coefficients, beam_weights):
    n_tm, n_feed = lax.axis_size("tm"), lax.axis_size("feed")
    turned = channelize(voltages, coefficients, n_tm)
    left = left_operand(turned, n_tm)
    return beams_power(left, beam_weights, n_feed)[None]


def fits(voltages, coefficients, beam_weights):
    n_tm, n_feed = lax.axis_size("tm"), lax.axis_size("feed")
    feeds_here, samples = voltages.shape
    frame_len = coefficients.shape[1]
    return (
        samples == frame_len
        and n_tm == INTEG
        and feeds_here % (16 * n_tm) == 0
        and frame_len % (256 * n_tm) == 0
        and beam_weights.shape[3] % (128 * n_feed) == 0
    )


def local(voltages, coefficients, beam_weights):
    plan = fast if fits(voltages, coefficients, beam_weights) else general
    return plan(voltages, coefficients, beam_weights)


def solution(mesh):
    placed = (P("feed", "tm"), P(), P("tm", "feed", None, None))
    return jax.shard_map(
        local, mesh=mesh, in_specs=placed, out_specs=P(None, "tm", "feed"), check_vma=False
    )
```
